512 devices in a mesh: seq: 64 (over z_hi, y, core), chan: 8 (over x, z_lo).
Axes of the slice: x: 4, y: 8, z: 8 (z_hi: 4, z_lo: 2; z = z_hi * 2 + z_lo), core: 2. Of those that a mesh axis runs over, the one named last changes fastest.
Arguments:
- inputs: bfloat16 [65536, 2048], P('seq', 'chan'), may hold values from -6 to 6
- out_grad: bfloat16 [65536, 2048], P('seq', 'chan'), may hold values from -6 to 6
- kernel: bfloat16 [64, 1024, 2048], P(None, 'seq', 'chan'), may hold values from -6 to 6
- inner_factor: bfloat16 [1024, 1024], replicated, may hold values from -0.1875 to 0.1875
- outer_factor: float32 [64, 64], replicated, may hold values from -0.75 to 0.75
- chan_blocks: bfloat16 [8, 256, 256], P('chan'), may hold values from -0.375 to 0.375
- chan_mixers: bfloat16 [256, 8, 8], replicated, may hold values from -2 to 2
Outputs:
- mixed: bfloat16 [65536, 2048], P('seq', 'chan')
- in_grad: bfloat16 [65536, 2048], P('seq', 'chan')
- kernel_grad: bfloat16 [64, 1024, 2048], P(None, 'seq', 'chan')
The draws below stay inside these ranges and needn't reach their ends.
All inputs are finite; a program needn't handle non-finite values.
Results may differ from the reference program's by a relative error of at most 0.014.
Values may be sent and summed in bfloat16 or wider, within the bound.
A program may use at most 64 MiB of HBM per device.

```python
import jax
import jax.numpy as jnp
from jax import lax

D = 2048
BLK = 1024
NCB = 8
GRID = 64
CB = 256
TOKENS = 65536


def steps_of(own_key, shape, pieces, smallest, top_value):
    loudness = 1.0
    for position, parts in pieces:
        steps = jax.random.uniform(jax.random.fold_in(jax.random.fold_in(own_key, 6), position), (parts,), jnp.float32, smallest / len(pieces), top_value / len(pieces))
        loudness = loudness * jnp.repeat(jnp.exp(steps), shape[position] // parts).reshape((-1,) + (1,) * (len(shape) - 1 - position))
    return loudness


def normal_values(rng, shape, scale, bound, split=(), dtype=jnp.bfloat16):
    level = steps_of(rng, shape, split, -0.22, 0.18) if split else 1.0
    drawn = jax.random.normal(rng, shape, jnp.float32) * scale * level
    return jnp.minimum(jnp.maximum(drawn, -bound), bound).astype(dtype)


def setup_inputs(seed: int = 0) -> dict:
    seeds = jax.random.split(jax.random.key(seed), 8)
    return {
        "inputs": normal_values(seeds[0], (TOKENS, D), 1.0, 6.0, ((0, 64), (1, 8))),
        "out_grad": normal_values(seeds[1], (TOKENS, D), 1.0, 6.0, ((0, 64), (1, 8))),
        "kernel": normal_values(seeds[2], (GRID, BLK, D), 1.0, 6.0, ((1, 64), (2, 8))),
        "inner_factor": normal_values(seeds[3], (BLK, BLK), BLK ** -0.5, 0.1875),
        "outer_factor": normal_values(seeds[4], (GRID, GRID), GRID ** -0.5, 0.75, (), jnp.float32),
        "chan_blocks": normal_values(seeds[5], (NCB, CB, CB), CB ** -0.5, 0.375, ((0, 8),)),
        "chan_mixers": normal_values(seeds[6], (CB, NCB, NCB), NCB ** -0.5, 2.0),
    }


HIGH = lax.Precision.HIGHEST


def reference(inputs, out_grad, kernel, inner_factor, outer_factor, chan_blocks, chan_mixers):
    f32 = jnp.float32
    bf16 = jnp.bfloat16
    grid_x = inputs.reshape(GRID, BLK, D).astype(f32)
    inner = inner_factor.astype(f32)
    gate = kernel.astype(f32)
    first = jnp.einsum('ijc,jk->ikc', grid_x, inner, precision=HIGH)
    second = jnp.einsum('ai,ijc->ajc', outer_factor, first, precision=HIGH)
    gated = second * gate
    back = jnp.einsum('ia,ijc->ajc', outer_factor, gated, precision=HIGH).astype(bf16)
    ymat = jnp.einsum('ijc,kj->ikc', back.astype(f32), inner, precision=HIGH).astype(bf16)
    yres = ymat.reshape(TOKENS, NCB, CB).astype(f32)
    pmat = jnp.einsum('tgm,gmn->tgn', yres, chan_blocks.astype(f32), precision=HIGH).astype(bf16)
    qmat = jnp.einsum('tgm,mhg->thm', pmat.astype(f32), chan_mixers.astype(f32), precision=HIGH).astype(bf16)
    qmat = lax.optimization_barrier(qmat)
    mixed = (inputs.astype(f32) + qmat.reshape(TOKENS, D).astype(f32)).astype(bf16)
    dq_res = out_grad.reshape(TOKENS, NCB, CB).astype(f32)
    dp_mat = jnp.einsum('thm,mhg->tgm', dq_res, chan_mixers.astype(f32), precision=HIGH).astype(bf16)
    dy_mat = jnp.einsum('tgn,gmn->tgm', dp_mat.astype(f32), chan_blocks.astype(f32), precision=HIGH).astype(bf16)
    dy_grid = dy_mat.reshape(GRID, BLK, D).astype(f32)
    dc_mat = jnp.einsum('ikc,kj->ijc', dy_grid, inner, precision=HIGH)
    dg_mat = jnp.einsum('ai,ijc->ajc', outer_factor, dc_mat, precision=HIGH)
    kernel_grad = (dg_mat * second).astype(bf16)
    da_mat = jnp.einsum('ai,ajc->ijc', outer_factor, dg_mat * gate, precision=HIGH).astype(bf16)
    dx_mat = jnp.einsum('ikc,jk->ijc', da_mat.astype(f32), inner, precision=HIGH)
    in_grad = (out_grad.astype(f32) + dx_mat.reshape(TOKENS, D)).astype(bf16)
    return mixed, in_grad, kernel_grad
```

```python
import jax
import jax.numpy as jnp
from jax import lax
from jax.experimental import pallas as pl
from jax.experimental.pallas import tpu as pltpu
from jax.sharding import PartitionSpec as P

MESH = pl.DeviceIdType.MESH
F32 = jnp.float32
BF16 = jnp.bfloat16

ZH, YC, NX, NZ, NQ = 4, 16, 4, 8, 8
PLANE = NX * NZ


def mm(a, b, dims=((1,), (0,))):
    return lax.dot_general(a, b, (dims, ((), ())), preferred_element_type=F32)


def iota(shape, dim):
    return lax.broadcasted_iota(jnp.int32, shape, dim)


def kernel(
    x_ref, og_ref, gate_ref, inner_ref, outer_ref, blocks_ref, mix_ref,
    mixed_ref, ingrad_ref, kgrad_ref,
    a_buf, e_buf, fz, fy, b_buf, cc, fp, fm, fq, fa, fs, fr,
    by, bs, ba, bq, bm, bd, da, bt, bu,
    k_mat, kt_mat, w_blk, w_mix, w_perm,
    send, recv,
):
    s = lax.axis_index("seq")
    q = lax.axis_index("chan")
    zh, yc = s // YC, s % YC
    xx, zl = q // 2, q % 2
    zz = zh * 2 + zl

    def dev(zh_, yc_, q_):
        return (zh_ * YC + yc_, q_)

    def yc_peer(d):
        y = (yc // 2 + d // 2) % 8
        return y * 2 + (yc + d) % 2

    def plane_peer(d):
        z = (zz + d // NX) % NZ
        return z // 2, ((xx + d) % NX) * 2 + z % 2

    def chan_peer(d):
        return ((xx + d // 2) % NX) * 2 + (zl + d) % 2

    def put(src, dst, stage, to):
        pltpu.make_async_remote_copy(
            src_ref=src, dst_ref=dst, send_sem=send.at[stage], recv_sem=recv.at[stage],
            device_id=to, device_id_type=MESH,
        ).start()

    near = dev(zh, yc_peer(1), q)

    def taken(part, stage):
        pltpu.make_async_remote_copy(
            src_ref=part, dst_ref=part, send_sem=send.at[stage], recv_sem=recv.at[stage],
            device_id=near, device_id_type=MESH,
        ).wait_recv()

    def sent(part, stage):
        pltpu.make_async_remote_copy(
            src_ref=part, dst_ref=part, send_sem=send.at[stage], recv_sem=recv.at[stage],
            device_id=near, device_id_type=MESH,
        ).wait_send()

    def loop(n, body, start=0):
        def step(i, carry):
            body(i)
            return carry

        lax.fori_loop(start, n, step, 0)

    def rows(i, n=256):
        return pl.ds(pl.multiple_of(i * n, n), n)

    barrier = pltpu.get_barrier_semaphore()

    def greet_yc(d):
        pl.semaphore_signal(barrier, inc=1, device_id=dev(zh, yc_peer(d), q), device_id_type=MESH)

    def greet_plane(d):
        z_, q_ = plane_peer(d)
        pl.semaphore_signal(barrier, inc=1, device_id=dev(z_, yc, q_), device_id_type=MESH)

    loop(PLANE, greet_plane, 1)
    loop(YC, greet_yc, 1)

    def first(i):
        tall = inner_ref[:, rows(i)]
        a_buf[i] = mm(tall, x_ref[...], ((0,), (0,))).astype(BF16)
        e_buf[i] = mm(tall, og_ref[...], ((0,), (0,))).astype(BF16).reshape(YC, 16, 256)

    for i in range(ZH):
        first(i)

    pl.semaphore_wait(barrier, PLANE - 1 + YC - 1)

    def f1z(d):
        to = (zh + d) % ZH
        put(a_buf.at[to], fz.at[zh], 0, dev(to, yc, q))

    def b1(d):
        to = yc_peer(d)
        put(e_buf.at[:, to], by.at[yc], 1, dev(zh, to, q))

    loop(ZH, f1z, 1)
    loop(YC, b1, 1)
    fz[zh] = a_buf[zh]
    by[yc] = e_buf[:, yc]

    spread = (iota((1024, 64), 0) // 16 == iota((1024, 64), 1)).astype(BF16)
    outer = outer_ref[...].astype(BF16)

    def factors(i):
        mine = (i * 16 + iota((256, 64), 0) // 16 == iota((256, 64), 1)).astype(BF16)
        same = iota((256, 1024), 0) % 16 == iota((256, 1024), 1) % 16
        one = mm(mm(mine, outer).astype(BF16), spread, ((1,), (1,)))
        k_mat[rows(i)] = jnp.where(same, one, 0.0).astype(BF16)
        two = mm(mm(mine, outer, ((1,), (1,))).astype(BF16), spread, ((1,), (1,)))
        kt_mat[rows(i)] = jnp.where(same, two, 0.0).astype(BF16)

    loop(4, factors)

    def wide(r):
        col, row = iota((256, 1024), 1), iota((256, 1024), 0)
        place = (col // 128 * 32 + col % 32 == row) & (col % 128 // 32 == r)
        w_blk[rows(r)] = mm(blocks_ref[0], place.astype(BF16)).astype(BF16)

    loop(4, wide)

    mix = mix_ref[pl.ds(pl.multiple_of(q * 256, 256), 256)]

    def mixers(i):
        row, col = i * 256 + iota((256, 256), 0), iota((256, 256), 1)
        pick = (col == row % 32 * 8 + row // 128).astype(BF16)
        own = mm(pick, mix).astype(BF16)
        group = (iota((8, 1024), 1) // 128 == iota((8, 1024), 0)).astype(BF16)
        full = mm(own, group)
        same = iota((256, 1024), 0) % 128 == iota((256, 1024), 1) % 128
        w_mix[rows(i)] = jnp.where(same, full, 0.0).astype(BF16)

    loop(4, mixers)

    def swap(i):
        row, col = i * 128 + iota((128, 512), 0), iota((128, 512), 1)
        w_perm[rows(i, 128)] = (
            (row // 128 == col % 128 // 32) & (row % 128 // 32 == col // 128) & (row % 32 == col % 32)
        ).astype(BF16)

    loop(4, swap)

    taken(fz.at[pl.ds(0, 3)], 0)

    def f1y(d):
        to = yc_peer(d)
        put(fz.at[:, rows(to, 16)], fy.at[:, yc], 2, dev(zh, to, q))

    loop(YC, f1y, 1)
    fy[:, yc] = fz[:, rows(yc, 16)]

    taken(by.at[pl.ds(0, YC - 1)], 1)
    for hi_q in range(2):
        lanes = slice(hi_q * 128, hi_q * 128 + 128)
        t = by[:, :, :, lanes].reshape(4, 4, ZH, 16, 128)
        t = jnp.concatenate([t[:, r].reshape(256, 128) for r in range(4)], axis=1)
        t = mm(t, w_perm[...]).astype(BF16)
        for lo in range(4):
            u = t[:, lo * 128 : lo * 128 + 128].reshape(4, ZH, 16, 128)
            for hi in range(4):
                bs[:, hi_q * 4 + lo, hi] = u[hi]

    def b3(d):
        z_, q_ = plane_peer(d)
        put(bs.at[z_, q_], ba.at[q * ZH + zh], 3, dev(z_, yc, q_))

    loop(PLANE, b3, 1)
    ba[q * ZH + zh] = bs[zh, q]

    taken(fy.at[:, pl.ds(0, YC - 1)], 2)

    def second(i):
        full = mm(k_mat[rows(i)], fy[...].reshape(1024, 256))
        b_buf[rows(i)] = full
        cc[rows(i)] = (full * gate_ref[rows(i)].astype(F32)).astype(BF16)

    loop(4, second)

    def back(i):
        t = mm(kt_mat[rows(i)], cc[...]).astype(BF16).reshape(4, 4, 16, 256)
        u = jnp.concatenate([t[:, r].reshape(64, 256) for r in range(4)], axis=1)
        p = mm(u, w_blk[...]).astype(BF16)
        for g in range(NQ):
            fp[g, rows(i, 64)] = p[:, g * 128 : g * 128 + 128]

    loop(4, back)

    def f4(d):
        to = chan_peer(d)
        put(fp.at[to], fm.at[q], 4, dev(zh, yc, to))

    loop(NQ, f4, 1)
    fm[q] = fp[q]

    taken(ba.at[pl.ds(0, PLANE - 1)], 3)
    t = jnp.concatenate([ba[h * ZH : h * ZH + ZH].reshape(256, 128) for h in range(NQ)], axis=1)
    t = mm(t, w_mix[...]).astype(BF16)
    for g in range(NQ):
        bq[g] = t[:, g * 128 : g * 128 + 128]

    def b5(d):
        to = chan_peer(d)
        put(bq.at[to], bm.at[q], 5, dev(zh, yc, to))

    loop(NQ, b5, 1)
    bm[q] = bq[q]

    taken(fm.at[pl.ds(0, 7)], 4)
    t = jnp.concatenate([fm[g] for g in range(NQ)], axis=1)
    t = mm(t, w_mix[...], ((1,), (1,))).astype(BF16)
    for h in range(NQ):
        fq[h] = t[:, h * 128 : h * 128 + 128].reshape(ZH, 4, 16, 128)

    def f6(d):
        z_, q_ = plane_peer(d)
        put(fq.at[q_, z_], fa.at[zh * NQ + q], 6, dev(z_, yc, q_))

    loop(PLANE, f6, 1)
    fa[zh * NQ + q] = fq[q, zh]

    taken(bm.at[pl.ds(0, 7)], 5)

    def unmix(i):
        t = jnp.concatenate([bm[g, rows(i, 64)] for g in range(NQ)], axis=1)
        t = mm(t, w_blk[...], ((1,), (1,))).astype(BF16)
        for r in range(4):
            bd[pl.ds(i * 4, 4), r] = t[:, r * 256 : r * 256 + 256].reshape(4, 16, 256)

    loop(4, unmix)

    def third(i):
        full = mm(k_mat[rows(i)], bd[...].reshape(1024, 256))
        kgrad_ref[rows(i)] = (full * b_buf[rows(i)]).astype(BF16)
        cc[rows(i)] = (full * gate_ref[rows(i)].astype(F32)).astype(BF16)

    loop(4, third)

    def fourth(i):
        da[i] = mm(kt_mat[rows(i)], cc[...]).astype(BF16).reshape(YC, 16, 256)

    loop(4, fourth)

    def b8y(d):
        to = yc_peer(d)
        put(da.at[:, to], bt.at[:, yc], 7, dev(zh, to, q))

    loop(YC, b8y, 1)
    bt[:, yc] = da[:, yc]

    taken(fa.at[pl.ds(0, PLANE - 1)], 6)
    held = fa[...].reshape(ZH, NQ, 64, 128)
    for hi_q in range(2):
        lanes = slice(hi_q * 128, hi_q * 128 + 128)
        t = jnp.concatenate([held[:, hi_q * 4 + lo].reshape(256, 128) for lo in range(4)], axis=1)
        t = mm(t, w_perm[...]).astype(BF16)
        for r in range(4):
            u = t[:, r * 128 : r * 128 + 128].reshape(ZH, 4, 16, 128)
            for hi in range(4):
                fs[hi * 4 + r, :, :, lanes] = u[:, hi]

    def f8(d):
        to = yc_peer(d)
        put(fs.at[to], fr.at[:, yc], 8, dev(zh, to, q))

    loop(YC, f8, 1)
    fr[:, yc] = fs[yc]

    taken(bt.at[:, pl.ds(0, YC - 1)], 7)

    def b8z(d):
        to = (zh + d) % ZH
        put(bt.at[to], bu.at[zh], 9, dev(to, yc, q))

    loop(ZH, b8z, 1)
    bu[zh] = bt[zh]

    taken(fr.at[:, pl.ds(0, YC - 1)], 8)

    def last_mixed(i):
        t = mm(inner_ref[rows(i)], fr[...].reshape(1024, 256))
        mixed_ref[rows(i)] = (x_ref[rows(i)].astype(F32) + t).astype(BF16)

    loop(4, last_mixed)

    taken(bu.at[pl.ds(0, 3)], 9)

    def last_grad(i):
        t = mm(inner_ref[rows(i)], bu[...].reshape(1024, 256))
        ingrad_ref[rows(i)] = (og_ref[rows(i)].astype(F32) + t).astype(BF16)

    loop(4, last_grad)

    sent(fz.at[pl.ds(0, 3)], 0)
    sent(by.at[pl.ds(0, YC - 1)], 1)
    sent(fy.at[:, pl.ds(0, YC - 1)], 2)
    sent(ba.at[pl.ds(0, PLANE - 1)], 3)
    sent(fm.at[pl.ds(0, 7)], 4)
    sent(bm.at[pl.ds(0, 7)], 5)
    sent(fa.at[pl.ds(0, PLANE - 1)], 6)
    sent(bt.at[:, pl.ds(0, YC - 1)], 7)
    sent(fr.at[:, pl.ds(0, YC - 1)], 8)
    sent(bu.at[pl.ds(0, 3)], 9)


def local(inputs, out_grad, kernel_gate, inner_factor, outer_factor, chan_blocks, chan_mixers):
    vmem = pl.BlockSpec(memory_space=pltpu.VMEM)
    full = jax.ShapeDtypeStruct((1024, 256), BF16)

    def buf(*shape, dtype=BF16):
        return pltpu.VMEM(shape, dtype)

    mixed, in_grad, kernel_grad = pl.pallas_call(
        kernel,
        out_shape=(full, full, full),
        in_specs=[vmem] * 7,
        out_specs=(vmem, vmem, vmem),
        scratch_shapes=[
            buf(ZH, 256, 256),
            buf(ZH, YC, 16, 256),
            buf(ZH, 256, 256),
            buf(ZH, YC, 16, 256),
            buf(1024, 256, dtype=F32),
            buf(1024, 256),
            buf(NQ, 256, 128),
            buf(NQ, 256, 128),
            buf(NQ, ZH, 4, 16, 128),
            buf(PLANE, 4, 16, 128),
            buf(YC, ZH, 16, 256),
            buf(ZH, YC, 16, 256),
            buf(YC, ZH, 16, 256),
            buf(ZH, NQ, 4, 16, 128),
            buf(PLANE, 4, 16, 128),
            buf(NQ, 256, 128),
            buf(NQ, 256, 128),
            buf(16, 4, 16, 256),
            buf(ZH, YC, 16, 256),
            buf(ZH, YC, 16, 256),
            buf(ZH, YC, 16, 256),
            buf(1024, 1024),
            buf(1024, 1024),
            buf(1024, 1024),
            buf(1024, 1024),
            buf(512, 512),
            pltpu.SemaphoreType.DMA((10,)),
            pltpu.SemaphoreType.DMA((10,)),
        ],
        compiler_params=pltpu.CompilerParams(
            collective_id=0, has_side_effects=True, vmem_limit_bytes=48 << 20
        ),
    )(
        inputs,
        out_grad,
        kernel_gate.reshape(1024, 256),
        inner_factor,
        outer_factor,
        chan_blocks,
        chan_mixers.reshape(2048, 8),
    )
    return mixed, in_grad, kernel_grad.reshape(64, 16, 256)


def solution(mesh):
    in_specs = (
        P("seq", "chan"),
        P("seq", "chan"),
        P(None, "seq", "chan"),
        P(),
        P(),
        P("chan", None, None),
        P(),
    )
    out_specs = (P("seq", "chan"), P("seq", "chan"), P(None, "seq", "chan"))
    return jax.shard_map(local, mesh=mesh, in_specs=in_specs, out_specs=out_specs, check_vma=False)
```

```python
import jax
import jax.numpy as jnp
from jax import lax
from jax.experimental import pallas as pl
from jax.experimental.pallas import tpu as pltpu
from jax.sharding import PartitionSpec as P

MESH = pl.DeviceIdType.MESH
F32 = jnp.float32
BF16 = jnp.bfloat16

ZH, YC, NX, NZ, NQ = 4, 16, 4, 8, 8
PLANE = NX * NZ
ORDER = (2, 1, 3, 0)


def mm(a, b, dims=((1,), (0,))):
    return lax.dot_general(a, b, (dims, ((), ())), preferred_element_type=F32)


def iota(shape, dim):
    return lax.broadcasted_iota(jnp.int32, shape, dim)


def kernel(
    x_hbm, og_hbm, gate_hbm, inner_hbm, outer_hbm, blocks_hbm, mix_hbm,
    mixed_hbm, ingrad_hbm, kgrad_hbm,
    a_buf, e_buf, fz, fy, b_buf, d_buf, cc, fp, fm, fq, fa, fs, fr,
    by, bs, ba, bq, bm, bd, da, bt, bu,
    k_mat, kt_mat,
    x_ref, og_ref, gate_ref, inner_ref, outer_ref, blocks_ref, mix_ref, vec_ref,
    mixed_ref, ingrad_ref, kgrad_ref,
    send, recv, load, store,
):
    s = lax.axis_index("seq")
    q = lax.axis_index("chan")
    zh, yc = s // YC, s % YC
    xx, zl = q // 2, q % 2
    zz = zh * 2 + zl

    def ahead(d):
        return (zh + d) % ZH

    def behind(d):
        return (zh + ZH - d) % ZH

    def dev(zh_, yc_, q_):
        return (zh_ * YC + yc_, q_)

    def yc_peer(d):
        y = (yc // 2 + d // 2) % 8
        return y * 2 + (yc + d) % 2

    def plane_peer(d):
        z = (zz + d // NX) % NZ
        return z // 2, ((xx + d) % NX) * 2 + z % 2

    def chan_peer(d):
        return ((xx + d // 2) % NX) * 2 + (zl + d) % 2

    def put(src, dst, stage, d, to):
        pltpu.make_async_remote_copy(
            src_ref=src, dst_ref=dst, send_sem=send.at[stage], recv_sem=recv.at[stage, d],
            device_id=to, device_id_type=MESH,
        ).start()

    near = dev(zh, yc_peer(1), q)

    def taken(part, stage, d):
        pltpu.make_async_remote_copy(
            src_ref=part, dst_ref=part, send_sem=send.at[stage], recv_sem=recv.at[stage, d],
            device_id=near, device_id_type=MESH,
        ).wait_recv()

    def sent(part, stage):
        pltpu.make_async_remote_copy(
            src_ref=part, dst_ref=part, send_sem=send.at[stage], recv_sem=recv.at[stage, 0],
            device_id=near, device_id_type=MESH,
        ).wait_send()

    def loop(n, body, start=0):
        def step(i, carry):
            body(i)
            return carry

        lax.fori_loop(start, n, step, 0)

    def rows(i, n=256):
        return pl.ds(pl.multiple_of(i * n, n), n)

    loads = [
        pltpu.make_async_copy(x_hbm, x_ref, load.at[0]),
        pltpu.make_async_copy(og_hbm, og_ref, load.at[1]),
    ]
    for i, d in enumerate(ORDER):
        loads.append(
            pltpu.make_async_copy(
                inner_hbm.at[:, rows(ahead(d))], inner_ref.at[:, rows(ahead(d))], load.at[2 + i]
            )
        )
    loads += [
        pltpu.make_async_copy(outer_hbm, outer_ref, load.at[6]),
        pltpu.make_async_copy(blocks_hbm, blocks_ref, load.at[7]),
        pltpu.make_async_copy(mix_hbm, mix_ref, load.at[8]),
        pltpu.make_async_copy(gate_hbm, gate_ref, load.at[9]),
    ]
    for copy in loads:
        copy.start()

    barrier = pltpu.get_barrier_semaphore()

    def greet_yc(d):
        pl.semaphore_signal(barrier, inc=1, device_id=dev(zh, yc_peer(d), q), device_id_type=MESH)

    def greet_plane(d):
        z_, q_ = plane_peer(d)
        pl.semaphore_signal(barrier, inc=1, device_id=dev(z_, yc, q_), device_id_type=MESH)

    loop(PLANE, greet_plane, 1)
    loop(YC, greet_yc, 1)

    def to_yc(src, dst, stage, d):
        def one(i):
            to = yc_peer(i)
            put(src(to), dst, stage, d, dev(zh, to, q))

        loop(YC, one, 1)

    def to_plane(src, dst, stage, d):
        def one(i):
            to = chan_peer(i)
            put(src(to), dst, stage, d, dev(ahead(d), yc, to))

        loop(NQ, one, 0 if d else 1)

    def to_chan(src, dst, stage, d):
        def one(i):
            to = chan_peer(i)
            put(src(to), dst, stage, d, dev(zh, yc, to))

        loop(NQ, one, 1)

    def swap(parts):
        group = iota(parts[0].shape, 1) // 32
        out = []
        for b in range(4):
            t = parts[b]
            for a in range(4):
                if a != b:
                    t = jnp.where(group == a, pltpu.roll(parts[a], (a - b) % 4 * 32, 1), t)
            out.append(t)
        return out

    loads[0].wait()
    loads[1].wait()
    for i, d in enumerate(ORDER):
        to = ahead(d)
        loads[2 + i].wait()
        tall = inner_ref[:, rows(to)]
        a_buf[to] = mm(tall, x_ref[...], ((0,), (0,))).astype(BF16)
        e_buf[to] = mm(tall, og_ref[...], ((0,), (0,))).astype(BF16).reshape(YC, 16, 256)
        if i == 0:
            pl.semaphore_wait(barrier, PLANE - 1 + YC - 1)
        if d:
            put(a_buf.at[to], fz.at[zh], 0, d, dev(to, yc, q))
        else:
            to_yc(lambda p: a_buf.at[zh, rows(p, 16)], fy.at[zh, yc], 2, 0)
            fy[zh, yc] = a_buf[zh, rows(yc, 16)]
        to_yc(lambda p, to=to: e_buf.at[to, p], by.at[yc, to], 1, d)
        by[yc, to] = e_buf[to, yc]

    for copy in loads[6:]:
        copy.wait()

    mine = (iota((256, 128), 0) == q * 32 + iota((256, 128), 1) % 32).astype(BF16)
    vec_ref[...] = mm(mix_ref[...].reshape(64, 256), mine)

    spread = (iota((1024, 64), 0) // 16 == iota((1024, 64), 1)).astype(BF16)
    outer = outer_ref[...].astype(BF16)

    def factors(i):
        mine = (i * 16 + iota((256, 64), 0) // 16 == iota((256, 64), 1)).astype(BF16)
        same = iota((256, 1024), 0) % 16 == iota((256, 1024), 1) % 16
        one = mm(mm(mine, outer).astype(BF16), spread, ((1,), (1,)))
        k_mat[rows(i)] = jnp.where(same, one, 0.0).astype(BF16)
        two = mm(mm(mine, outer, ((1,), (1,))).astype(BF16), spread, ((1,), (1,)))
        kt_mat[rows(i)] = jnp.where(same, two, 0.0).astype(BF16)

    def b2(d):
        to = ahead(d)
        taken(by.at[pl.ds(0, YC - 1), 0], 1, d)
        for hi_q in range(2):
            t = by[:, to, :, hi_q * 128 : hi_q * 128 + 128].astype(F32).reshape(4, 4, 16, 128)
            u = swap([t[:, r].reshape(64, 128) for r in range(4)])
            for lo in range(4):
                bs[to, hi_q * 4 + lo] = u[lo].astype(BF16)
        to_plane(lambda p: bs.at[to, p], ba.at[q * ZH + zh], 3, d)
        if not d:
            ba[q * ZH + zh] = bs[zh, q]

    def f1y(d):
        of = behind(d)
        taken(fz.at[0], 0, d)
        to_yc(lambda p: fz.at[of, rows(p, 16)], fy.at[of, yc], 2, d)
        fy[of, yc] = fz[of, rows(yc, 16)]

    for i, d in enumerate(ORDER):
        b2(d)
        if d:
            f1y(d)
        if i == 0:
            loop(4, factors)

    def outer_sum(out, part, of, first):
        def one(i):
            t = mm(k_mat[rows(i), rows(of)], part)
            out[rows(i)] = t if first else out[rows(i)] + t

        loop(4, one)

    def f2(d, first):
        of = behind(d)
        taken(fy.at[0, pl.ds(0, YC - 1)], 2, d)
        outer_sum(b_buf, fy[of].reshape(256, 256), of, first)

    def mixed_down(src, dst, flip):
        def one(i):
            parts = [src(g, rows(i, 16)).astype(F32) for g in range(NQ)]
            for h in range(NQ):
                t = None
                for g in range(NQ):
                    at = g * NQ + h if flip else h * NQ + g
                    u = parts[g] * vec_ref[at : at + 1]
                    t = u if t is None else t + u
                dst(h, rows(i, 16), t.astype(BF16))

        loop(4, one)

    def b4(d):
        of = behind(d)
        taken(ba.at[pl.ds(0, NQ if d else NQ - 1)], 3, d)

        def store(g, at, t):
            bq[g, of, at] = t

        mixed_down(lambda h, at: ba[h * ZH + of, at], store, True)
        to_chan(lambda p: bq.at[p, of], bm.at[q, of], 5, d)
        bm[q, of] = bq[q, of]

    f2(0, True)
    for d in ORDER[:3]:
        f2(d, False)
        b4(d)
    b4(0)

    def gated(src):
        def one(i):
            gate = gate_ref[rows(i, 16)].reshape(256, 256).astype(F32)
            cc[rows(i)] = (src[rows(i)] * gate).astype(BF16)

        loop(4, one)

    gated(b_buf)
    for d in ORDER:
        to = ahead(d)
        t = mm(kt_mat[rows(to)], cc[...]).astype(BF16)
        t = mm(t, blocks_ref[0]).reshape(4, 4, 16, 256)
        for hi_q in range(2):
            u = swap([t[:, r, :, hi_q * 128 : hi_q * 128 + 128].reshape(64, 128) for r in range(4)])
            for lo in range(4):
                fp[hi_q * 4 + lo, to] = u[lo].astype(BF16)
        to_chan(lambda p: fp.at[p, to], fm.at[q, to], 4, d)
        fm[q, to] = fp[q, to]

    def f5(d):
        to = ahead(d)
        taken(fm.at[pl.ds(0, NQ - 1), 0], 4, d)

        def store(h, at, t):
            fq[h, to, at] = t

        mixed_down(lambda g, at: fm[g, to, at], store, False)
        to_plane(lambda p: fq.at[p, to], fa.at[zh * NQ + q], 6, d)
        if not d:
            fa[zh * NQ + q] = fq[q, zh]

    def b6(d, first):
        of = behind(d)
        taken(bm.at[pl.ds(0, NQ - 1), 0], 5, d)
        half = []
        for hi_q in range(2):
            half.append(swap([bm[hi_q * 4 + lo, of].astype(F32) for lo in range(4)]))
        for r in range(4):
            t = jnp.concatenate([half[0][r], half[1][r]], axis=1).astype(BF16)
            t = mm(t, blocks_ref[0], ((1,), (1,))).astype(BF16).reshape(4, 16, 256)
            for hi in range(4):
                bd[pl.ds(hi * 64 + r * 16, 16)] = t[hi]
        outer_sum(d_buf, bd[...], of, first)

    for i, d in enumerate(ORDER):
        f5(d)
        b6(d, i == 0)

    gated(d_buf)
    for d in ORDER:
        to = ahead(d)
        da[to] = mm(kt_mat[rows(to)], cc[...]).astype(BF16).reshape(YC, 16, 256)
        to_yc(lambda p: da.at[to, p], bt.at[to, yc], 7, d)
        bt[to, yc] = da[to, yc]

    def kernel_grad(i):
        kgrad_ref[rows(i)] = (d_buf[rows(i)] * b_buf[rows(i)]).astype(BF16)

    loop(4, kernel_grad)
    out_kgrad = pltpu.make_async_copy(kgrad_ref, kgrad_hbm, store.at[8])
    out_kgrad.start()

    def f7(d):
        of = behind(d)
        taken(fa.at[pl.ds(0, NQ if d else NQ - 1)], 6, d)
        for hi_q in range(2):
            u = swap([fa[of * NQ + hi_q * 4 + lo].astype(F32) for lo in range(4)])
            for r in range(4):
                t = u[r].astype(BF16).reshape(4, 16, 128)
                for hi in range(4):
                    fs[of, hi * 4 + r, :, hi_q * 128 : hi_q * 128 + 128] = t[hi]
        to_yc(lambda p: fs.at[of, p], fr.at[of, yc], 8, d)
        fr[of, yc] = fs[of, yc]

    def b8z(d):
        to = ahead(d)
        taken(bt.at[0, pl.ds(0, YC - 1)], 7, d)
        if d:
            put(bt.at[to], bu.at[zh], 9, d, dev(to, yc, q))
        else:
            bu[zh] = bt[zh]

    for d in ORDER:
        f7(d)
        b8z(d)

    def stored(i, at):
        src, dst = ((mixed_ref, mixed_hbm), (ingrad_ref, ingrad_hbm))[at]
        return pltpu.make_async_copy(src.at[rows(i)], dst.at[rows(i)], store.at[at * 4 + i])

    def last(out, base, part, of, first, final):
        def one(i):
            t = mm(inner_ref[rows(i), rows(of)], part)
            if not first:
                t = out[rows(i)] + t
            else:
                t = base[rows(i)].astype(F32) + t
            if final is None:
                out[rows(i)] = t
            else:
                (mixed_ref, ingrad_ref)[final][rows(i)] = t.astype(BF16)
                stored(i, final).start()

        loop(4, one)

    last(d_buf, og_ref, bu[zh].reshape(256, 256), zh, True, None)
    for i, d in enumerate(ORDER):
        of = behind(d)
        taken(fr.at[0, pl.ds(0, YC - 1)], 8, d)
        last(b_buf, x_ref, fr[of].reshape(256, 256), of, i == 0, 0 if i == 3 else None)
    for i, d in enumerate(ORDER[:3]):
        of = behind(d)
        taken(bu.at[0], 9, d)
        last(d_buf, og_ref, bu[of].reshape(256, 256), of, False, 1 if i == 2 else None)

    sent(fz.at[pl.ds(0, 3)], 0)
    sent(by.at[pl.ds(0, YC - 1)], 1)
    sent(fy.at[:, pl.ds(0, YC - 1)], 2)
    sent(ba.at[pl.ds(0, PLANE - 1)], 3)
    sent(fm.at[pl.ds(0, NQ - 1)], 4)
    sent(bm.at[pl.ds(0, NQ - 1)], 5)
    sent(fa.at[pl.ds(0, PLANE - 1)], 6)
    sent(bt.at[:, pl.ds(0, YC - 1)], 7)
    sent(fr.at[:, pl.ds(0, YC - 1)], 8)
    sent(bu.at[pl.ds(0, 3)], 9)
    out_kgrad.wait()
    for i in range(4):
        stored(i, 0).wait()
        stored(i, 1).wait()


def local(inputs, out_grad, kernel_gate, inner_factor, outer_factor, chan_blocks, chan_mixers):
    full = jax.ShapeDtypeStruct((1024, 256), BF16)

    def buf(*shape, dtype=BF16):
        return pltpu.VMEM(shape, dtype)

    mixed, in_grad, kernel_grad = pl.pallas_call(
        kernel,
        out_shape=(full, full, full),
        in_specs=[pl.BlockSpec(memory_space=pl.ANY)] * 7,
        out_specs=[pl.BlockSpec(memory_space=pl.ANY)] * 3,
        scratch_shapes=[
            buf(ZH, 256, 256),
            buf(ZH, YC, 16, 256),
            buf(ZH, 256, 256),
            buf(ZH, YC, 16, 256),
            buf(1024, 256, dtype=F32),
            buf(1024, 256, dtype=F32),
            buf(1024, 256),
            buf(NQ, ZH, 64, 128),
            buf(NQ, ZH, 64, 128),
            buf(NQ, ZH, 64, 128),
            buf(PLANE, 64, 128),
            buf(ZH, YC, 16, 256),
            buf(ZH, YC, 16, 256),
            buf(YC, ZH, 16, 256),
            buf(ZH, NQ, 64, 128),
            buf(PLANE, 64, 128),
            buf(NQ, ZH, 64, 128),
            buf(NQ, ZH, 64, 128),
            buf(256, 256),
            buf(ZH, YC, 16, 256),
            buf(ZH, YC, 16, 256),
            buf(ZH, YC, 16, 256),
            buf(1024, 1024),
            buf(1024, 1024),
            buf(1024, 256),
            buf(1024, 256),
            buf(64, 16, 256),
            buf(1024, 1024),
            buf(64, 64, dtype=F32),
            buf(1, 256, 256),
            buf(8, 8, 256),
            buf(64, 128, dtype=F32),
            buf(1024, 256),
            buf(1024, 256),
            buf(1024, 256),
            pltpu.SemaphoreType.DMA((10,)),
            pltpu.SemaphoreType.DMA((10, ZH)),
            pltpu.SemaphoreType.DMA((10,)),
            pltpu.SemaphoreType.DMA((9,)),
        ],
        compiler_params=pltpu.CompilerParams(
            collective_id=0, has_side_effects=True, vmem_limit_bytes=62 << 20
        ),
    )(
        inputs,
        out_grad,
        kernel_gate,
        inner_factor,
        outer_factor,
        chan_blocks,
        jnp.transpose(chan_mixers, (1, 2, 0)),
    )
    return mixed, in_grad, kernel_grad.reshape(64, 16, 256)


def solution(mesh):
    in_specs = (
        P("seq", "chan"),
        P("seq", "chan"),
        P(None, "seq", "chan"),
        P(),
        P(),
        P("chan", None, None),
        P(),
    )
    out_specs = (P("seq", "chan"), P("seq", "chan"), P(None, "seq", "chan"))
    return jax.shard_map(local, mesh=mesh, in_specs=in_specs, out_specs=out_specs, check_vma=False)
```

```python
import jax
import jax.numpy as jnp
from jax import lax
from jax.experimental import pallas as pl
from jax.experimental.pallas import tpu as pltpu
from jax.sharding import PartitionSpec as P

MESH = pl.DeviceIdType.MESH
F32 = jnp.float32
BF16 = jnp.bfloat16

ZH, YC, NX, NZ, NQ = 4, 16, 4, 8, 8
PLANE = NX * NZ
ORDER = (1, 3, 2, 0)


def mm(a, b, dims=((1,), (0,))):
    return lax.dot_general(a, b, (dims, ((), ())), preferred_element_type=F32)


def iota(shape, dim):
    return lax.broadcasted_iota(jnp.int32, shape, dim)


def kernel(
    x_hbm, og_hbm, gate_hbm, inner_hbm, outer_hbm, blocks_hbm, mix_hbm,
    mixed_hbm, ingrad_hbm, kgrad_hbm,
    a_buf, e_buf, fz, fy, b_buf, d_buf, cc, fp, fm, fq, fa, fs, fr,
    by, bs, ba, bq, bm, bd, da, bt, bu,
    k_mat, kt_mat,
    x_ref, og_ref, gate_ref, inner_ref, outer_ref, blocks_ref, mix_ref, vec_ref,
    mixed_ref, ingrad_ref, kgrad_ref,
    send, recv, load, store,
):
    s = lax.axis_index("seq")
    q = lax.axis_index("chan")
    zh, yc = s >> 4, s & 15
    xx, zl = q >> 1, q & 1

    def ahead(d):
        return (zh + d) & (ZH - 1)

    def behind(d):
        return (zh + ZH - d) & (ZH - 1)

    def dev(zh_, yc_, q_):
        return (zh_ * YC + yc_, q_)

    def put(src, dst, stage, d, to):
        pltpu.make_async_remote_copy(
            src_ref=src, dst_ref=dst, send_sem=send.at[stage], recv_sem=recv.at[stage, d],
            device_id=to, device_id_type=MESH,
        ).start()

    near = (s ^ 1, q)

    def taken(part, stage, d):
        pltpu.make_async_remote_copy(
            src_ref=part, dst_ref=part, send_sem=send.at[stage], recv_sem=recv.at[stage, d],
            device_id=near, device_id_type=MESH,
        ).wait_recv()

    def sent(part, stage):
        pltpu.make_async_remote_copy(
            src_ref=part, dst_ref=part, send_sem=send.at[stage], recv_sem=recv.at[stage, 0],
            device_id=near, device_id_type=MESH,
        ).wait_send()

    def loop(n, body, start=0):
        def step(i, carry):
            body(i)
            return carry

        lax.fori_loop(start, n, step, 0)

    def rows(i, n=256):
        return pl.ds(pl.multiple_of(i * n, n), n)

    loads = [
        pltpu.make_async_copy(x_hbm, x_ref, load.at[0]),
        pltpu.make_async_copy(og_hbm, og_ref, load.at[1]),
    ]
    for i, d in enumerate(ORDER):
        loads.append(
            pltpu.make_async_copy(
                inner_hbm.at[:, rows(ahead(d))], inner_ref.at[:, rows(ahead(d))], load.at[2 + i]
            )
        )
    loads += [
        pltpu.make_async_copy(outer_hbm, outer_ref, load.at[6]),
        pltpu.make_async_copy(blocks_hbm, blocks_ref, load.at[7]),
        pltpu.make_async_copy(mix_hbm, mix_ref, load.at[8]),
        pltpu.make_async_copy(gate_hbm, gate_ref, load.at[9]),
    ]
    for copy in loads:
        copy.start()

    barrier = pltpu.get_barrier_semaphore()

    def greet(seq, chan):
        pl.semaphore_signal(barrier, inc=1, device_id=(seq, chan), device_id_type=MESH)

    for z in range(1, ZH):
        loop(NQ, lambda i, z=z: greet(s ^ z * YC, q ^ i))
    loop(NQ, lambda i: greet(s, q ^ i), 1)
    loop(YC, lambda i: greet(s ^ i, q), 1)

    def to_yc(src, dst, stage, d):
        def one(i):
            put(src(yc ^ i), dst, stage, d, (s ^ i, q))

        loop(YC, one, 1)

    def to_plane(src, dst, stage, d):
        def one(i):
            to = q ^ i
            put(src(to), dst, stage, d, dev(ahead(d), yc, to))

        loop(NQ, one, 0 if d else 1)

    def to_chan(src, dst, stage, d):
        def one(i):
            to = q ^ i
            put(src(to), dst, stage, d, dev(zh, yc, to))

        loop(NQ, one, 1)

    def swap(parts):
        group = iota(parts[0].shape, 1) // 32
        out = []
        for b in range(4):
            t = parts[b]
            for a in range(4):
                if a != b:
                    t = jnp.where(group == a, pltpu.roll(parts[a], (a - b) % 4 * 32, 1), t)
            out.append(t)
        return out

    loads[0].wait()
    loads[1].wait()
    for i, d in enumerate(ORDER):
        to = ahead(d)
        loads[2 + i].wait()
        tall = inner_ref[:, rows(to)]
        a_buf[to] = mm(tall, x_ref[...], ((0,), (0,))).astype(BF16)
        e_buf[to] = mm(tall, og_ref[...], ((0,), (0,))).astype(BF16).reshape(YC, 16, 256)
        if i == 0:
            pl.semaphore_wait(barrier, PLANE - 1 + YC - 1)
        if d:
            put(a_buf.at[to], fz.at[zh], 0, d, dev(to, yc, q))
        else:
            to_yc(lambda p: a_buf.at[zh, rows(p, 16)], fy.at[zh, yc], 2, 0)
            fy[zh, yc] = a_buf[zh, rows(yc, 16)]
        to_yc(lambda p, to=to: e_buf.at[to, p], by.at[yc, to], 1, d)
        by[yc, to] = e_buf[to, yc]

    for copy in loads[6:]:
        copy.wait()

    mine = (iota((256, 128), 0) == q * 32 + iota((256, 128), 1) % 32).astype(BF16)
    vec_ref[...] = mm(mix_ref[...].reshape(64, 256), mine)

    spread = (iota((1024, 64), 0) // 16 == iota((1024, 64), 1)).astype(BF16)
    outer = outer_ref[...].astype(BF16)

    def factors(i):
        mine = (i * 16 + iota((256, 64), 0) // 16 == iota((256, 64), 1)).astype(BF16)
        same = iota((256, 1024), 0) % 16 == iota((256, 1024), 1) % 16
        one = mm(mm(mine, outer).astype(BF16), spread, ((1,), (1,)))
        k_mat[rows(i)] = jnp.where(same, one, 0.0).astype(BF16)
        two = mm(mm(mine, outer, ((1,), (1,))).astype(BF16), spread, ((1,), (1,)))
        kt_mat[rows(i)] = jnp.where(same, two, 0.0).astype(BF16)

    def b2(d):
        to = ahead(d)
        taken(by.at[pl.ds(0, YC - 1), 0], 1, d)
        for hi_q in range(2):
            t = by[:, to, :, hi_q * 128 : hi_q * 128 + 128].astype(F32).reshape(4, 4, 16, 128)
            u = swap([t[:, r].reshape(64, 128) for r in range(4)])
            for lo in range(4):
                bs[to, hi_q * 4 + lo] = u[lo].astype(BF16)
        to_plane(lambda p: bs.at[to, p], ba.at[q * ZH + zh], 3, d)
        if not d:
            ba[q * ZH + zh] = bs[zh, q]

    def f1y(d):
        of = behind(d)
        taken(fz.at[0], 0, d)
        to_yc(lambda p: fz.at[of, rows(p, 16)], fy.at[of, yc], 2, d)
        fy[of, yc] = fz[of, rows(yc, 16)]

    for i, d in enumerate(ORDER):
        b2(d)
        if d:
            f1y(d)
        if i == 0:
            loop(4, factors)

    def outer_sum(out, part, of, first):
        def one(i):
            t = mm(k_mat[rows(i), rows(of)], part)
            out[rows(i)] = t if first else out[rows(i)] + t

        loop(4, one)

    def f2(d, first):
        of = behind(d)
        taken(fy.at[0, pl.ds(0, YC - 1)], 2, d)
        outer_sum(b_buf, fy[of].reshape(256, 256), of, first)

    def mixed_down(src, dst, flip):
        def one(i):
            parts = [src(g, rows(i, 16)).astype(F32) for g in range(NQ)]
            for h in range(NQ):
                t = None
                for g in range(NQ):
                    at = g * NQ + h if flip else h * NQ + g
                    u = parts[g] * vec_ref[at : at + 1]
                    t = u if t is None else t + u
                dst(h, rows(i, 16), t.astype(BF16))

        loop(4, one)

    def b4(d):
        of = behind(d)
        taken(ba.at[pl.ds(0, NQ if d else NQ - 1)], 3, d)

        def store(g, at, t):
            bq[g, of, at] = t

        mixed_down(lambda h, at: ba[h * ZH + of, at], store, True)
        to_chan(lambda p: bq.at[p, of], bm.at[q, of], 5, d)
        bm[q, of] = bq[q, of]

    f2(0, True)
    for d in ORDER[:3]:
        f2(d, False)
        b4(d)
    b4(0)

    def gated(src):
        def one(i):
            gate = gate_ref[rows(i, 16)].reshape(256, 256).astype(F32)
            cc[rows(i)] = (src[rows(i)] * gate).astype(BF16)

        loop(4, one)

    gated(b_buf)
    for d in ORDER:
        to = ahead(d)
        t = mm(kt_mat[rows(to)], cc[...]).astype(BF16)
        t = mm(t, blocks_ref[0]).reshape(4, 4, 16, 256)
        for hi_q in range(2):
            u = swap([t[:, r, :, hi_q * 128 : hi_q * 128 + 128].reshape(64, 128) for r in range(4)])
            for lo in range(4):
                fp[hi_q * 4 + lo, to] = u[lo].astype(BF16)
        to_chan(lambda p: fp.at[p, to], fm.at[q, to], 4, d)
        fm[q, to] = fp[q, to]

    def f5(d):
        to = ahead(d)
        taken(fm.at[pl.ds(0, NQ - 1), 0], 4, d)

        def store(h, at, t):
            fq[h, to, at] = t

        mixed_down(lambda g, at: fm[g, to, at], store, False)
        to_plane(lambda p: fq.at[p, to], fa.at[zh * NQ + q], 6, d)
        if not d:
            fa[zh * NQ + q] = fq[q, zh]

    def b6(d, first):
        of = behind(d)
        taken(bm.at[pl.ds(0, NQ - 1), 0], 5, d)
        half = []
        for hi_q in range(2):
            half.append(swap([bm[hi_q * 4 + lo, of].astype(F32) for lo in range(4)]))
        for r in range(4):
            t = jnp.concatenate([half[0][r], half[1][r]], axis=1).astype(BF16)
            t = mm(t, blocks_ref[0], ((1,), (1,))).astype(BF16).reshape(4, 16, 256)
            for hi in range(4):
                bd[pl.ds(hi * 64 + r * 16, 16)] = t[hi]
        outer_sum(d_buf, bd[...], of, first)

    for i, d in enumerate(ORDER):
        f5(d)
        b6(d, i == 0)

    gated(d_buf)
    for d in ORDER:
        to = ahead(d)
        da[to] = mm(kt_mat[rows(to)], cc[...]).astype(BF16).reshape(YC, 16, 256)
        to_yc(lambda p: da.at[to, p], bt.at[to, yc], 7, d)
        bt[to, yc] = da[to, yc]

    def kernel_grad(i):
        kgrad_ref[rows(i)] = (d_buf[rows(i)] * b_buf[rows(i)]).astype(BF16)

    loop(4, kernel_grad)
    out_kgrad = pltpu.make_async_copy(kgrad_ref, kgrad_hbm, store.at[8])
    out_kgrad.start()

    def f7(d):
        of = behind(d)
        taken(fa.at[pl.ds(0, NQ if d else NQ - 1)], 6, d)
        for hi_q in range(2):
            u = swap([fa[of * NQ + hi_q * 4 + lo].astype(F32) for lo in range(4)])
            for r in range(4):
                t = u[r].astype(BF16).reshape(4, 16, 128)
                for hi in range(4):
                    fs[of, hi * 4 + r, :, hi_q * 128 : hi_q * 128 + 128] = t[hi]
        to_yc(lambda p: fs.at[of, p], fr.at[of, yc], 8, d)
        fr[of, yc] = fs[of, yc]

    def b8z(d):
        to = ahead(d)
        taken(bt.at[0, pl.ds(0, YC - 1)], 7, d)
        if d:
            put(bt.at[to], bu.at[zh], 9, d, dev(to, yc, q))
        else:
            bu[zh] = bt[zh]

    for d in ORDER:
        f7(d)
        b8z(d)

    def stored(i, at):
        src, dst = ((mixed_ref, mixed_hbm), (ingrad_ref, ingrad_hbm))[at]
        return pltpu.make_async_copy(src.at[rows(i)], dst.at[rows(i)], store.at[at * 4 + i])

    def last(out, base, part, of, first, final):
        def one(i):
            t = mm(inner_ref[rows(i), rows(of)], part)
            if not first:
                t = out[rows(i)] + t
            else:
                t = base[rows(i)].astype(F32) + t
            if final is None:
                out[rows(i)] = t
            else:
                (mixed_ref, ingrad_ref)[final][rows(i)] = t.astype(BF16)
                stored(i, final).start()

        loop(4, one)

    last(d_buf, og_ref, bu[zh].reshape(256, 256), zh, True, None)
    for i, d in enumerate(ORDER):
        of = behind(d)
        taken(fr.at[0, pl.ds(0, YC - 1)], 8, d)
        last(b_buf, x_ref, fr[of].reshape(256, 256), of, i == 0, 0 if i == 3 else None)
    for i, d in enumerate([d for d in ORDER if d]):
        of = behind(d)
        taken(bu.at[0], 9, d)
        last(d_buf, og_ref, bu[of].reshape(256, 256), of, False, 1 if i == 2 else None)

    sent(fz.at[pl.ds(0, 3)], 0)
    sent(by.at[pl.ds(0, YC - 1)], 1)
    sent(fy.at[:, pl.ds(0, YC - 1)], 2)
    sent(ba.at[pl.ds(0, PLANE - 1)], 3)
    sent(fm.at[pl.ds(0, NQ - 1)], 4)
    sent(bm.at[pl.ds(0, NQ - 1)], 5)
    sent(fa.at[pl.ds(0, PLANE - 1)], 6)
    sent(bt.at[:, pl.ds(0, YC - 1)], 7)
    sent(fr.at[:, pl.ds(0, YC - 1)], 8)
    sent(bu.at[pl.ds(0, 3)], 9)
    out_kgrad.wait()
    for i in range(4):
        stored(i, 0).wait()
        stored(i, 1).wait()


def hand_on(a_src, b_src, c_src, a_dst, b_dst, c_dst, held, come, go):
    pairs = ((c_src, c_dst), (a_src, a_dst), (b_src, b_dst))
    into = [pltpu.make_async_copy(p[0], held.at[i], come.at[i]) for i, p in enumerate(pairs)]
    out = [pltpu.make_async_copy(held.at[i], p[1], go.at[i]) for i, p in enumerate(pairs)]
    for copy in into:
        copy.start()
    for one, two in zip(into, out):
        one.wait()
        two.start()
    for copy in out:
        copy.wait()


def local(inputs, out_grad, kernel_gate, inner_factor, outer_factor, chan_blocks, chan_mixers):
    full = jax.ShapeDtypeStruct((1024, 256), BF16)

    def buf(*shape, dtype=BF16):
        return pltpu.VMEM(shape, dtype)

    mixed, in_grad, kernel_grad = pl.pallas_call(
        kernel,
        out_shape=(full, full, full),
        in_specs=[pl.BlockSpec(memory_space=pl.ANY)] * 7,
        out_specs=[pl.BlockSpec(memory_space=pl.ANY)] * 3,
        scratch_shapes=[
            buf(ZH, 256, 256),
            buf(ZH, YC, 16, 256),
            buf(ZH, 256, 256),
            buf(ZH, YC, 16, 256),
            buf(1024, 256, dtype=F32),
            buf(1024, 256, dtype=F32),
            buf(1024, 256),
            buf(NQ, ZH, 64, 128),
            buf(NQ, ZH, 64, 128),
            buf(NQ, ZH, 64, 128),
            buf(PLANE, 64, 128),
            buf(ZH, YC, 16, 256),
            buf(ZH, YC, 16, 256),
            buf(YC, ZH, 16, 256),
            buf(ZH, NQ, 64, 128),
            buf(PLANE, 64, 128),
            buf(NQ, ZH, 64, 128),
            buf(NQ, ZH, 64, 128),
            buf(256, 256),
            buf(ZH, YC, 16, 256),
            buf(ZH, YC, 16, 256),
            buf(ZH, YC, 16, 256),
            buf(1024, 1024),
            buf(1024, 1024),
            buf(1024, 256),
            buf(1024, 256),
            buf(64, 16, 256),
            buf(1024, 1024),
            buf(64, 64, dtype=F32),
            buf(1, 256, 256),
            buf(8, 8, 256),
            buf(64, 128, dtype=F32),
            buf(1024, 256),
            buf(1024, 256),
            buf(1024, 256),
            pltpu.SemaphoreType.DMA((10,)),
            pltpu.SemaphoreType.DMA((10, ZH)),
            pltpu.SemaphoreType.DMA((10,)),
            pltpu.SemaphoreType.DMA((9,)),
        ],
        compiler_params=pltpu.CompilerParams(
            collective_id=0, has_side_effects=True, vmem_limit_bytes=62 << 20
        ),
    )(
        inputs,
        out_grad,
        kernel_gate,
        inner_factor,
        outer_factor,
        chan_blocks,
        jnp.transpose(chan_mixers, (1, 2, 0)),
    )
    mixed, in_grad, kernel_grad = pl.pallas_call(
        hand_on,
        out_shape=(full, full, full),
        in_specs=[pl.BlockSpec(memory_space=pl.ANY)] * 3,
        out_specs=[pl.BlockSpec(memory_space=pl.ANY)] * 3,
        scratch_shapes=[buf(3, 1024, 256), pltpu.SemaphoreType.DMA((3,)), pltpu.SemaphoreType.DMA((3,))],
        compiler_params=pltpu.CompilerParams(vmem_limit_bytes=62 << 20),
    )(mixed, in_grad, kernel_grad)
    return mixed, in_grad, kernel_grad.reshape(64, 16, 256)


def solution(mesh):
    in_specs = (
        P("seq", "chan"),
        P("seq", "chan"),
        P(None, "seq", "chan"),
        P(),
        P(),
        P("chan", None, None),
        P(),
    )
    out_specs = (P("seq", "chan"), P("seq", "chan"), P(None, "seq", "chan"))
    return jax.shard_map(local, mesh=mesh, in_specs=in_specs, out_specs=out_specs, check_vma=False)
```

```python
import jax
import jax.numpy as jnp
from jax import lax
from jax.experimental import pallas as pl
from jax.experimental.pallas import tpu as pltpu
from jax.sharding import PartitionSpec as P

MESH = pl.DeviceIdType.MESH
F32 = jnp.float32
BF16 = jnp.bfloat16

ZH, YC, NX, NZ, NQ = 4, 16, 4, 8, 8
PLANE = NX * NZ
ORDER = (1, 3, 2, 0)


def mm(a, b, dims=((1,), (0,))):
    return lax.dot_general(a, b, (dims, ((), ())), preferred_element_type=F32)


def iota(shape, dim):
    return lax.broadcasted_iota(jnp.int32, shape, dim)


def kernel(
    x_hbm, og_hbm, gate_hbm, inner_hbm, outer_hbm, blocks_hbm, mix_hbm,
    mixed_hbm, ingrad_hbm, kgrad_hbm,
    a_buf, e_buf, fz, fy, b_buf, d_buf, cc, fp, fm, fq, fa, fs, fr,
    by, bs, ba, bq, bm, bd, da, bt, bu,
    k_mat, kt_mat,
    both_ref, gate_ref, inner_ref, outer_ref, blocks_ref, mix_ref, vec_ref,
    mixed_ref, ingrad_ref, kgrad_ref,
    send, recv, load, store,
):
    s = lax.axis_index("seq")
    q = lax.axis_index("chan")
    zh, yc = s >> 4, s & 15
    xx, zl = q >> 1, q & 1

    x_ref = both_ref.at[:, pl.ds(0, 256)]
    og_ref = both_ref.at[:, pl.ds(256, 256)]

    def ahead(d):
        return (zh + d) & (ZH - 1)

    def behind(d):
        return (zh + ZH - d) & (ZH - 1)

    def dev(zh_, yc_, q_):
        return (zh_ * YC + yc_, q_)

    def put(src, dst, stage, d, to):
        pltpu.make_async_remote_copy(
            src_ref=src, dst_ref=dst, send_sem=send.at[stage], recv_sem=recv.at[stage, d],
            device_id=to, device_id_type=MESH,
        ).start()

    near = (s ^ 1, q)

    def taken(part, stage, d):
        pltpu.make_async_remote_copy(
            src_ref=part, dst_ref=part, send_sem=send.at[stage], recv_sem=recv.at[stage, d],
            device_id=near, device_id_type=MESH,
        ).wait_recv()

    def sent(part, stage):
        pltpu.make_async_remote_copy(
            src_ref=part, dst_ref=part, send_sem=send.at[stage], recv_sem=recv.at[stage, 0],
            device_id=near, device_id_type=MESH,
        ).wait_send()

    def loop(n, body, start=0):
        def step(i, carry):
            body(i)
            return carry

        lax.fori_loop(start, n, step, 0)

    def rows(i, n=256):
        return pl.ds(pl.multiple_of(i * n, n), n)

    loads = [
        pltpu.make_async_copy(x_hbm, x_ref, load.at[0]),
        pltpu.make_async_copy(og_hbm, og_ref, load.at[1]),
    ]
    for i, d in enumerate(ORDER):
        loads.append(
            pltpu.make_async_copy(
                inner_hbm.at[:, rows(ahead(d))], inner_ref.at[:, rows(ahead(d))], load.at[2 + i]
            )
        )
    loads += [
        pltpu.make_async_copy(outer_hbm, outer_ref, load.at[6]),
        pltpu.make_async_copy(blocks_hbm, blocks_ref, load.at[7]),
        pltpu.make_async_copy(mix_hbm, mix_ref, load.at[8]),
        pltpu.make_async_copy(gate_hbm, gate_ref, load.at[9]),
    ]
    for copy in loads:
        copy.start()

    barrier = pltpu.get_barrier_semaphore()

    def greet(seq, chan):
        pl.semaphore_signal(barrier, inc=1, device_id=(seq, chan), device_id_type=MESH)

    for z in range(1, ZH):
        loop(NQ, lambda i, z=z: greet(s ^ z * YC, q ^ i))
    loop(NQ, lambda i: greet(s, q ^ i), 1)
    loop(YC, lambda i: greet(s ^ i, q), 1)

    def to_yc(src, dst, stage, d):
        def one(i):
            put(src(yc ^ i), dst, stage, d, (s ^ i, q))

        loop(YC, one, 1)

    def to_plane(src, dst, stage, d):
        def one(i):
            to = q ^ i
            put(src(to), dst, stage, d, dev(ahead(d), yc, to))

        loop(NQ, one, 0 if d else 1)

    def to_chan(src, dst, stage, d):
        def one(i):
            to = q ^ i
            put(src(to), dst, stage, d, dev(zh, yc, to))

        loop(NQ, one, 1)

    def swap(parts):
        group = iota(parts[0].shape, 1) // 32
        out = []
        for b in range(4):
            t = parts[b]
            for a in range(4):
                if a != b:
                    t = jnp.where(group == a, pltpu.roll(parts[a], (a - b) % 4 * 32, 1), t)
            out.append(t)
        return out

    loads[0].wait()
    loads[1].wait()
    for i, d in enumerate(ORDER):
        to = ahead(d)
        loads[2 + i].wait()
        tall = inner_ref[:, rows(to)]
        t = mm(tall, both_ref[...], ((0,), (0,))).astype(BF16)
        a_buf[to] = t[:, :256]
        e_buf[to] = t[:, 256:].reshape(YC, 16, 256)
        if i == 0:
            pl.semaphore_wait(barrier, PLANE - 1 + YC - 1)
        if d:
            put(a_buf.at[to], fz.at[zh], 0, d, dev(to, yc, q))
        else:
            to_yc(lambda p: a_buf.at[zh, rows(p, 16)], fy.at[zh, yc], 2, 0)
            fy[zh, yc] = a_buf[zh, rows(yc, 16)]
        to_yc(lambda p, to=to: e_buf.at[to, p], by.at[yc, to], 1, d)
        by[yc, to] = e_buf[to, yc]

    for copy in loads[6:]:
        copy.wait()

    mine = (iota((256, 128), 0) == q * 32 + iota((256, 128), 1) % 32).astype(BF16)
    vec_ref[...] = mm(mix_ref[...].reshape(64, 256), mine)

    spread = (iota((1024, 64), 0) // 16 == iota((1024, 64), 1)).astype(BF16)
    outer = outer_ref[...].astype(BF16)

    def factors(i):
        mine = (i * 16 + iota((256, 64), 0) // 16 == iota((256, 64), 1)).astype(BF16)
        same = iota((256, 1024), 0) % 16 == iota((256, 1024), 1) % 16
        one = mm(mm(mine, outer).astype(BF16), spread, ((1,), (1,)))
        k_mat[rows(i)] = jnp.where(same, one, 0.0).astype(BF16)
        two = mm(mm(mine, outer, ((1,), (1,))).astype(BF16), spread, ((1,), (1,)))
        kt_mat[rows(i)] = jnp.where(same, two, 0.0).astype(BF16)

    def b2(d):
        to = ahead(d)
        taken(by.at[pl.ds(0, YC - 1), 0], 1, d)
        for hi_q in range(2):
            t = by[:, to, :, hi_q * 128 : hi_q * 128 + 128].astype(F32).reshape(4, 4, 16, 128)
            u = swap([t[:, r].reshape(64, 128) for r in range(4)])
            for lo in range(4):
                bs[to, hi_q * 4 + lo] = u[lo].astype(BF16)
        to_plane(lambda p: bs.at[to, p], ba.at[q * ZH + zh], 3, d)
        if not d:
            ba[q * ZH + zh] = bs[zh, q]

    def f1y(d):
        of = behind(d)
        taken(fz.at[0], 0, d)
        to_yc(lambda p: fz.at[of, rows(p, 16)], fy.at[of, yc], 2, d)
        fy[of, yc] = fz[of, rows(yc, 16)]

    for i, d in enumerate(ORDER):
        b2(d)
        if d:
            f1y(d)
        if i == 0:
            loop(4, factors)

    def outer_sum(out, part, of, first, final=False):
        def one(i):
            t = mm(k_mat[rows(i), rows(of)], part)
            t = t if first else out[rows(i)] + t
            out[rows(i)] = t
            if final:
                cc[rows(i)] = (t * gate_ref[rows(i, 16)].reshape(256, 256).astype(F32)).astype(BF16)

        loop(4, one)

    def f2(d, first, final=False):
        of = behind(d)
        taken(fy.at[0, pl.ds(0, YC - 1)], 2, d)
        outer_sum(b_buf, fy[of].reshape(256, 256), of, first, final)

    def mixed_down(src, dst, flip):
        def one(i):
            parts = [src(g, rows(i, 16)).astype(F32) for g in range(NQ)]
            for h in range(NQ):
                t = None
                for g in range(NQ):
                    at = g * NQ + h if flip else h * NQ + g
                    u = parts[g] * vec_ref[at : at + 1]
                    t = u if t is None else t + u
                dst(h, rows(i, 16), t.astype(BF16))

        loop(4, one)

    def b4(d):
        of = behind(d)
        taken(ba.at[pl.ds(0, NQ if d else NQ - 1)], 3, d)

        def store(g, at, t):
            bq[g, of, at] = t

        mixed_down(lambda h, at: ba[h * ZH + of, at], store, True)
        to_chan(lambda p: bq.at[p, of], bm.at[q, of], 5, d)
        bm[q, of] = bq[q, of]

    f2(0, True)
    for d in ORDER[:3]:
        f2(d, False, d == 2)
        b4(d)
    b4(0)

    for d in ORDER:
        to = ahead(d)
        t = mm(kt_mat[rows(to)], cc[...]).astype(BF16)
        t = mm(t, blocks_ref[0]).reshape(4, 4, 16, 256)
        for hi_q in range(2):
            u = swap([t[:, r, :, hi_q * 128 : hi_q * 128 + 128].reshape(64, 128) for r in range(4)])
            for lo in range(4):
                fp[hi_q * 4 + lo, to] = u[lo].astype(BF16)
        to_chan(lambda p: fp.at[p, to], fm.at[q, to], 4, d)
        fm[q, to] = fp[q, to]

    def f5(d):
        to = ahead(d)
        taken(fm.at[pl.ds(0, NQ - 1), 0], 4, d)

        def store(h, at, t):
            fq[h, to, at] = t

        mixed_down(lambda g, at: fm[g, to, at], store, False)
        to_plane(lambda p: fq.at[p, to], fa.at[zh * NQ + q], 6, d)
        if not d:
            fa[zh * NQ + q] = fq[q, zh]

    def b6(d, first, final):
        of = behind(d)
        taken(bm.at[pl.ds(0, NQ - 1), 0], 5, d)
        half = []
        for hi_q in range(2):
            half.append(swap([bm[hi_q * 4 + lo, of].astype(F32) for lo in range(4)]))
        for r in range(4):
            t = jnp.concatenate([half[0][r], half[1][r]], axis=1).astype(BF16)
            t = mm(t, blocks_ref[0], ((1,), (1,))).astype(BF16).reshape(4, 16, 256)
            for hi in range(4):
                bd[pl.ds(hi * 64 + r * 16, 16)] = t[hi]
        outer_sum(d_buf, bd[...], of, first, final)

    for i, d in enumerate(ORDER):
        b6(d, i == 0, i == 3)
        f5(d)

    for d in ORDER:
        to = ahead(d)
        da[to] = mm(kt_mat[rows(to)], cc[...]).astype(BF16).reshape(YC, 16, 256)
        to_yc(lambda p: da.at[to, p], bt.at[to, yc], 7, d)
        bt[to, yc] = da[to, yc]

    def kernel_grad(i):
        kgrad_ref[rows(i)] = (d_buf[rows(i)] * b_buf[rows(i)]).astype(BF16)

    loop(4, kernel_grad)
    out_kgrad = pltpu.make_async_copy(kgrad_ref, kgrad_hbm, store.at[8])
    out_kgrad.start()

    def f7(d):
        of = behind(d)
        taken(fa.at[pl.ds(0, NQ if d else NQ - 1)], 6, d)
        for hi_q in range(2):
            u = swap([fa[of * NQ + hi_q * 4 + lo].astype(F32) for lo in range(4)])
            for r in range(4):
                t = u[r].astype(BF16).reshape(4, 16, 128)
                for hi in range(4):
                    fs[of, hi * 4 + r, :, hi_q * 128 : hi_q * 128 + 128] = t[hi]
        to_yc(lambda p: fs.at[of, p], fr.at[of, yc], 8, d)
        fr[of, yc] = fs[of, yc]

    def b8z(d):
        to = ahead(d)
        taken(bt.at[0, pl.ds(0, YC - 1)], 7, d)
        if d:
            put(bt.at[to], bu.at[zh], 9, d, dev(to, yc, q))
        else:
            bu[zh] = bt[zh]

    for d in ORDER:
        b8z(d)
        f7(d)

    def stored(i, at):
        src, dst = ((mixed_ref, mixed_hbm), (ingrad_ref, ingrad_hbm))[at]
        return pltpu.make_async_copy(src.at[rows(i)], dst.at[rows(i)], store.at[at * 4 + i])

    def last(out, base, part, of, first, final):
        def one(i):
            t = mm(inner_ref[rows(i), rows(of)], part)
            if not first:
                t = out[rows(i)] + t
            else:
                t = base[rows(i)].astype(F32) + t
            if final is None:
                out[rows(i)] = t
            else:
                (mixed_ref, ingrad_ref)[final][rows(i)] = t.astype(BF16)
                stored(i, final).start()

        loop(4, one)

    def f9(d, first, final):
        of = behind(d)
        taken(fr.at[0, pl.ds(0, YC - 1)], 8, d)
        last(b_buf, x_ref, fr[of].reshape(256, 256), of, first, final)

    def b9(d, final):
        of = behind(d)
        taken(bu.at[0], 9, d)
        last(d_buf, og_ref, bu[of].reshape(256, 256), of, False, final)

    last(d_buf, og_ref, bu[zh].reshape(256, 256), zh, True, None)
    f9(1, True, None)
    f9(3, False, None)
    b9(1, None)
    f9(2, False, None)
    b9(3, None)
    f9(0, False, 0)
    b9(2, 1)

    sent(fz.at[pl.ds(0, 3)], 0)
    sent(by.at[pl.ds(0, YC - 1)], 1)
    sent(fy.at[:, pl.ds(0, YC - 1)], 2)
    sent(ba.at[pl.ds(0, PLANE - 1)], 3)
    sent(fm.at[pl.ds(0, NQ - 1)], 4)
    sent(bm.at[pl.ds(0, NQ - 1)], 5)
    sent(fa.at[pl.ds(0, PLANE - 1)], 6)
    sent(bt.at[:, pl.ds(0, YC - 1)], 7)
    sent(fr.at[:, pl.ds(0, YC - 1)], 8)
    sent(bu.at[pl.ds(0, 3)], 9)
    out_kgrad.wait()
    for i in range(4):
        stored(i, 0).wait()
        stored(i, 1).wait()


def hand_on(a_src, b_src, c_src, a_dst, b_dst, c_dst, held, come, go):
    pairs = [
        (src.at[pl.ds(k * 256, 256)], dst.at[pl.ds(k * 256, 256)])
        for src, dst in ((c_src, c_dst), (a_src, a_dst), (b_src, b_dst))
        for k in range(4)
    ]
    into = [pltpu.make_async_copy(p[0], held.at[i], come.at[i]) for i, p in enumerate(pairs)]
    out = [pltpu.make_async_copy(held.at[i], p[1], go.at[i]) for i, p in enumerate(pairs)]
    for copy in into:
        copy.start()
    for one, two in zip(into, out):
        one.wait()
        two.start()
    for copy in out:
        copy.wait()


def local(inputs, out_grad, kernel_gate, inner_factor, outer_factor, chan_blocks, chan_mixers):
    full = jax.ShapeDtypeStruct((1024, 256), BF16)

    def buf(*shape, dtype=BF16):
        return pltpu.VMEM(shape, dtype)

    mixed, in_grad, kernel_grad = pl.pallas_call(
        kernel,
        out_shape=(full, full, full),
        in_specs=[pl.BlockSpec(memory_space=pl.ANY)] * 7,
        out_specs=[pl.BlockSpec(memory_space=pl.ANY)] * 3,
        scratch_shapes=[
            buf(ZH, 256, 256),
            buf(ZH, YC, 16, 256),
            buf(ZH, 256, 256),
            buf(ZH, YC, 16, 256),
            buf(1024, 256, dtype=F32),
            buf(1024, 256, dtype=F32),
            buf(1024, 256),
            buf(NQ, ZH, 64, 128),
            buf(NQ, ZH, 64, 128),
            buf(NQ, ZH, 64, 128),
            buf(PLANE, 64, 128),
            buf(ZH, YC, 16, 256),
            buf(ZH, YC, 16, 256),
            buf(YC, ZH, 16, 256),
            buf(ZH, NQ, 64, 128),
            buf(PLANE, 64, 128),
            buf(NQ, ZH, 64, 128),
            buf(NQ, ZH, 64, 128),
            buf(256, 256),
            buf(ZH, YC, 16, 256),
            buf(ZH, YC, 16, 256),
            buf(ZH, YC, 16, 256),
            buf(1024, 1024),
            buf(1024, 1024),
            buf(1024, 512),
            buf(64, 16, 256),
            buf(1024, 1024),
            buf(64, 64, dtype=F32),
            buf(1, 256, 256),
            buf(8, 8, 256),
            buf(64, 128, dtype=F32),
            buf(1024, 256),
            buf(1024, 256),
            buf(1024, 256),
            pltpu.SemaphoreType.DMA((10,)),
            pltpu.SemaphoreType.DMA((10, ZH)),
            pltpu.SemaphoreType.DMA((10,)),
            pltpu.SemaphoreType.DMA((9,)),
        ],
        compiler_params=pltpu.CompilerParams(
            collective_id=0, has_side_effects=True, vmem_limit_bytes=62 << 20
        ),
    )(
        inputs,
        out_grad,
        kernel_gate,
        inner_factor,
        outer_factor,
        chan_blocks,
        jnp.transpose(chan_mixers, (1, 2, 0)),
    )
    mixed, in_grad, kernel_grad = pl.pallas_call(
        hand_on,
        out_shape=(full, full, full),
        in_specs=[pl.BlockSpec(memory_space=pl.ANY)] * 3,
        out_specs=[pl.BlockSpec(memory_space=pl.ANY)] * 3,
        scratch_shapes=[buf(12, 256, 256), pltpu.SemaphoreType.DMA((12,)), pltpu.SemaphoreType.DMA((12,))],
        compiler_params=pltpu.CompilerParams(vmem_limit_bytes=62 << 20),
    )(mixed, in_grad, kernel_grad)
    return mixed, in_grad, kernel_grad.reshape(64, 16, 256)


def solution(mesh):
    in_specs = (
        P("seq", "chan"),
        P("seq", "chan"),
        P(None, "seq", "chan"),
        P(),
        P(),
        P("chan", None, None),
        P(),
    )
    out_specs = (P("seq", "chan"), P("seq", "chan"), P(None, "seq", "chan"))
    return jax.shard_map(local, mesh=mesh, in_specs=in_specs, out_specs=out_specs, check_vma=False)
```

```python
import jax
import jax.numpy as jnp
from jax import lax
from jax.experimental import pallas as pl
from jax.experimental.pallas import tpu as pltpu
from jax.sharding import PartitionSpec as P

MESH = pl.DeviceIdType.MESH
F32 = jnp.float32
BF16 = jnp.bfloat16

ZH, YC, NX, NZ, NQ = 4, 16, 4, 8, 8
PLANE = NX * NZ
ORDER = (1, 3, 2, 0)


def mm(a, b, dims=((1,), (0,))):
    return lax.dot_general(a, b, (dims, ((), ())), preferred_element_type=F32)


def iota(shape, dim):
    return lax.broadcasted_iota(jnp.int32, shape, dim)


def kernel(
    x_hbm, og_hbm, gate_hbm, inner_hbm, outer_hbm, blocks_hbm, mix_hbm,
    mixed_hbm, ingrad_hbm, kgrad_hbm,
    a_buf, e_buf, fz, fy, b_buf, d_buf, cc, fp, fm, fq, fa, fs, fr,
    by, bs, ba, bq, bm, bd, da, bt, bu,
    k_mat, kt_mat,
    both_ref, gate_ref, inner_ref, outer_ref, blocks_ref, mix_ref, vec_ref,
    mixed_ref, ingrad_ref, kgrad_ref,
    send, recv, load, store,
):
    s = lax.axis_index("seq")
    q = lax.axis_index("chan")
    zh, yc = s >> 4, s & 15
    xx, zl = q >> 1, q & 1

    x_ref = both_ref.at[:, pl.ds(0, 256)]
    og_ref = both_ref.at[:, pl.ds(256, 256)]

    def ahead(d):
        return (zh + d) & (ZH - 1)

    def behind(d):
        return (zh + ZH - d) & (ZH - 1)

    def dev(zh_, yc_, q_):
        return (zh_ * YC + yc_, q_)

    def put(src, dst, stage, d, to):
        pltpu.make_async_remote_copy(
            src_ref=src, dst_ref=dst, send_sem=send.at[stage], recv_sem=recv.at[stage, d],
            device_id=to, device_id_type=MESH,
        ).start()

    near = (s ^ 1, q)

    def taken(part, stage, d):
        pltpu.make_async_remote_copy(
            src_ref=part, dst_ref=part, send_sem=send.at[stage], recv_sem=recv.at[stage, d],
            device_id=near, device_id_type=MESH,
        ).wait_recv()

    def sent(part, stage):
        pltpu.make_async_remote_copy(
            src_ref=part, dst_ref=part, send_sem=send.at[stage], recv_sem=recv.at[stage, 0],
            device_id=near, device_id_type=MESH,
        ).wait_send()

    def loop(n, body, start=0):
        def step(i, carry):
            body(i)
            return carry

        lax.fori_loop(start, n, step, 0)

    def rows(i, n=256):
        return pl.ds(pl.multiple_of(i * n, n), n)

    loads = [
        pltpu.make_async_copy(x_hbm, x_ref, load.at[0]),
        pltpu.make_async_copy(og_hbm, og_ref, load.at[1]),
    ]
    for i, d in enumerate(ORDER):
        loads.append(
            pltpu.make_async_copy(
                inner_hbm.at[:, rows(ahead(d))], inner_ref.at[:, rows(ahead(d))], load.at[2 + i]
            )
        )
    loads += [
        pltpu.make_async_copy(outer_hbm, outer_ref, load.at[6]),
        pltpu.make_async_copy(blocks_hbm, blocks_ref, load.at[7]),
        pltpu.make_async_copy(mix_hbm, mix_ref, load.at[8]),
        pltpu.make_async_copy(gate_hbm, gate_ref, load.at[9]),
    ]
    for copy in loads:
        copy.start()

    barrier = pltpu.get_barrier_semaphore()

    def greet(seq, chan):
        pl.semaphore_signal(barrier, inc=1, device_id=(seq, chan), device_id_type=MESH)

    for z in range(1, ZH):
        loop(NQ, lambda i, z=z: greet(s ^ z * YC, q ^ i))
    loop(NQ, lambda i: greet(s, q ^ i), 1)
    loop(YC, lambda i: greet(s ^ i, q), 1)

    def to_yc(src, dst, stage, d):
        def one(i):
            put(src(yc ^ i), dst, stage, d, (s ^ i, q))

        loop(YC, one, 1)

    def to_plane(src, dst, stage, d):
        def one(i):
            to = q ^ i
            put(src(to), dst, stage, d, dev(ahead(d), yc, to))

        loop(NQ, one, 0 if d else 1)

    def to_chan(src, dst, stage, d):
        def one(i):
            to = q ^ i
            put(src(to), dst, stage, d, dev(zh, yc, to))

        loop(NQ, one, 1)

    def swap(parts):
        group = iota(parts[0].shape, 1) // 32
        out = []
        for b in range(4):
            t = parts[b]
            for a in range(4):
                if a != b:
                    t = jnp.where(group == a, pltpu.roll(parts[a], (a - b) % 4 * 32, 1), t)
            out.append(t)
        return out

    loads[0].wait()
    loads[1].wait()
    for i, d in enumerate(ORDER):
        to = ahead(d)
        loads[2 + i].wait()
        tall = inner_ref[:, rows(to)]
        t = mm(tall, both_ref[...], ((0,), (0,))).astype(BF16)
        a_buf[to] = t[:, :256]
        e_buf[to] = t[:, 256:].reshape(YC, 16, 256)
        if i == 0:
            pl.semaphore_wait(barrier, PLANE - 1 + YC - 1)
        if d:
            put(a_buf.at[to], fz.at[zh], 0, d, dev(to, yc, q))
        else:
            to_yc(lambda p: a_buf.at[zh, rows(p, 16)], fy.at[zh, yc], 2, 0)
            fy[zh, yc] = a_buf[zh, rows(yc, 16)]
        to_yc(lambda p, to=to: e_buf.at[to, p], by.at[yc, to], 1, d)
        by[yc, to] = e_buf[to, yc]

    for copy in loads[6:]:
        copy.wait()

    mine = (iota((256, 128), 0) == q * 32 + iota((256, 128), 1) % 32).astype(BF16)
    vec_ref[...] = mm(mix_ref[...].reshape(64, 256), mine)

    spread = (iota((1024, 64), 0) // 16 == iota((1024, 64), 1)).astype(BF16)
    outer = outer_ref[...].astype(BF16)

    def factors(i):
        mine = (i * 16 + iota((256, 64), 0) // 16 == iota((256, 64), 1)).astype(BF16)
        same = iota((256, 1024), 0) % 16 == iota((256, 1024), 1) % 16
        one = mm(mm(mine, outer).astype(BF16), spread, ((1,), (1,)))
        k_mat[rows(i)] = jnp.where(same, one, 0.0).astype(BF16)
        two = mm(mm(mine, outer, ((1,), (1,))).astype(BF16), spread, ((1,), (1,)))
        kt_mat[rows(i)] = jnp.where(same, two, 0.0).astype(BF16)

    def b2(d):
        to = ahead(d)
        taken(by.at[pl.ds(0, YC - 1), 0], 1, d)
        for hi_q in range(2):
            t = by[:, to, :, hi_q * 128 : hi_q * 128 + 128].astype(F32).reshape(4, 4, 16, 128)
            u = swap([t[:, r].reshape(64, 128) for r in range(4)])
            for lo in range(4):
                bs[to, hi_q * 4 + lo] = u[lo].astype(BF16)
        to_plane(lambda p: bs.at[to, p], ba.at[q * ZH + zh], 3, d)
        if not d:
            ba[q * ZH + zh] = bs[zh, q]

    def f1y(d):
        of = behind(d)
        taken(fz.at[0], 0, d)
        to_yc(lambda p: fz.at[of, rows(p, 16)], fy.at[of, yc], 2, d)
        fy[of, yc] = fz[of, rows(yc, 16)]

    for i, d in enumerate(ORDER):
        b2(d)
        if d:
            f1y(d)
        if i == 1:
            loop(4, factors)

    def outer_sum(out, part, of, first, final=False):
        def one(i):
            t = mm(k_mat[rows(i), rows(of)], part)
            t = t if first else out[rows(i)] + t
            out[rows(i)] = t
            if final:
                cc[rows(i)] = (t * gate_ref[rows(i, 16)].reshape(256, 256).astype(F32)).astype(BF16)

        loop(4, one)

    def f2(d, first, final=False):
        of = behind(d)
        taken(fy.at[0, pl.ds(0, YC - 1)], 2, d)
        outer_sum(b_buf, fy[of].reshape(256, 256), of, first, final)

    def mixed_down(src, dst, flip):
        def one(i):
            parts = [src(g, rows(i, 16)).astype(F32) for g in range(NQ)]
            for h in range(NQ):
                t = None
                for g in range(NQ):
                    at = g * NQ + h if flip else h * NQ + g
                    u = parts[g] * vec_ref[at : at + 1]
                    t = u if t is None else t + u
                dst(h, rows(i, 16), t.astype(BF16))

        loop(4, one)

    def b4(d):
        of = behind(d)
        taken(ba.at[pl.ds(0, NQ if d else NQ - 1)], 3, d)

        def store(g, at, t):
            bq[g, of, at] = t

        mixed_down(lambda h, at: ba[h * ZH + of, at], store, True)
        to_chan(lambda p: bq.at[p, of], bm.at[q, of], 5, d)
        bm[q, of] = bq[q, of]

    f2(0, True)
    for d in ORDER[:3]:
        f2(d, False, d == 2)
        b4(d)
    b4(0)

    for d in ORDER:
        to = ahead(d)
        t = mm(kt_mat[rows(to)], cc[...]).astype(BF16)
        t = mm(t, blocks_ref[0]).reshape(4, 4, 16, 256)
        for hi_q in range(2):
            u = swap([t[:, r, :, hi_q * 128 : hi_q * 128 + 128].reshape(64, 128) for r in range(4)])
            for lo in range(4):
                fp[hi_q * 4 + lo, to] = u[lo].astype(BF16)
        to_chan(lambda p: fp.at[p, to], fm.at[q, to], 4, d)
        fm[q, to] = fp[q, to]

    def f5(d):
        to = ahead(d)
        taken(fm.at[pl.ds(0, NQ - 1), 0], 4, d)

        def store(h, at, t):
            fq[h, to, at] = t

        mixed_down(lambda g, at: fm[g, to, at], store, False)
        to_plane(lambda p: fq.at[p, to], fa.at[zh * NQ + q], 6, d)
        if not d:
            fa[zh * NQ + q] = fq[q, zh]

    def b6(d, first, final):
        of = behind(d)
        taken(bm.at[pl.ds(0, NQ - 1), 0], 5, d)
        half = []
        for hi_q in range(2):
            half.append(swap([bm[hi_q * 4 + lo, of].astype(F32) for lo in range(4)]))
        for r in range(4):
            t = jnp.concatenate([half[0][r], half[1][r]], axis=1).astype(BF16)
            t = mm(t, blocks_ref[0], ((1,), (1,))).astype(BF16).reshape(4, 16, 256)
            for hi in range(4):
                bd[pl.ds(hi * 64 + r * 16, 16)] = t[hi]
        outer_sum(d_buf, bd[...], of, first, final)

    for i, d in enumerate(ORDER):
        b6(d, i == 0, i == 3)
        f5(d)

    for d in ORDER:
        to = ahead(d)
        da[to] = mm(kt_mat[rows(to)], cc[...]).astype(BF16).reshape(YC, 16, 256)
        to_yc(lambda p: da.at[to, p], bt.at[to, yc], 7, d)
        bt[to, yc] = da[to, yc]

    def kernel_grad(i):
        kgrad_ref[rows(i)] = (d_buf[rows(i)] * b_buf[rows(i)]).astype(BF16)

    loop(4, kernel_grad)
    out_kgrad = pltpu.make_async_copy(kgrad_ref, kgrad_hbm, store.at[8])
    out_kgrad.start()

    def f7(d):
        of = behind(d)
        taken(fa.at[pl.ds(0, NQ if d else NQ - 1)], 6, d)
        for hi_q in range(2):
            u = swap([fa[of * NQ + hi_q * 4 + lo].astype(F32) for lo in range(4)])
            for r in range(4):
                t = u[r].astype(BF16).reshape(4, 16, 128)
                for hi in range(4):
                    fs[of, hi * 4 + r, :, hi_q * 128 : hi_q * 128 + 128] = t[hi]
        to_yc(lambda p: fs.at[of, p], fr.at[of, yc], 8, d)
        fr[of, yc] = fs[of, yc]

    def b8z(d):
        to = ahead(d)
        taken(bt.at[0, pl.ds(0, YC - 1)], 7, d)
        if d:
            put(bt.at[to], bu.at[zh], 9, d, dev(to, yc, q))
        else:
            bu[zh] = bt[zh]

    for d in ORDER:
        b8z(d)
        f7(d)

    def stored(i, at):
        src, dst = ((mixed_ref, mixed_hbm), (ingrad_ref, ingrad_hbm))[at]
        return pltpu.make_async_copy(src.at[rows(i)], dst.at[rows(i)], store.at[at * 4 + i])

    def last(out, base, part, of, first, final):
        def one(i):
            t = mm(inner_ref[rows(i), rows(of)], part)
            if not first:
                t = out[rows(i)] + t
            else:
                t = base[rows(i)].astype(F32) + t
            if final is None:
                out[rows(i)] = t
            else:
                (mixed_ref, ingrad_ref)[final][rows(i)] = t.astype(BF16)
                stored(i, final).start()

        loop(4, one)

    def f9(d, first, final):
        of = behind(d)
        taken(fr.at[0, pl.ds(0, YC - 1)], 8, d)
        last(b_buf, x_ref, fr[of].reshape(256, 256), of, first, final)

    def b9(d, final):
        of = behind(d)
        taken(bu.at[0], 9, d)
        last(d_buf, og_ref, bu[of].reshape(256, 256), of, False, final)

    last(d_buf, og_ref, bu[zh].reshape(256, 256), zh, True, None)
    f9(1, True, None)
    f9(3, False, None)
    b9(1, None)
    f9(2, False, None)
    b9(3, None)
    f9(0, False, 0)
    b9(2, 1)

    sent(fz.at[pl.ds(0, 3)], 0)
    sent(by.at[pl.ds(0, YC - 1)], 1)
    sent(fy.at[:, pl.ds(0, YC - 1)], 2)
    sent(ba.at[pl.ds(0, PLANE - 1)], 3)
    sent(fm.at[pl.ds(0, NQ - 1)], 4)
    sent(bm.at[pl.ds(0, NQ - 1)], 5)
    sent(fa.at[pl.ds(0, PLANE - 1)], 6)
    sent(bt.at[:, pl.ds(0, YC - 1)], 7)
    sent(fr.at[:, pl.ds(0, YC - 1)], 8)
    sent(bu.at[pl.ds(0, 3)], 9)
    out_kgrad.wait()
    for i in range(4):
        stored(i, 0).wait()
        stored(i, 1).wait()


def hand_on(a_src, b_src, c_src, a_dst, b_dst, c_dst, held, come, go):
    pairs = [
        (src.at[pl.ds(k * 256, 256)], dst.at[pl.ds(k * 256, 256)])
        for src, dst in ((c_src, c_dst), (a_src, a_dst), (b_src, b_dst))
        for k in range(4)
    ]
    into = [pltpu.make_async_copy(p[0], held.at[i], come.at[i]) for i, p in enumerate(pairs)]
    out = [pltpu.make_async_copy(held.at[i], p[1], go.at[i]) for i, p in enumerate(pairs)]
    for copy in into:
        copy.start()
    for one, two in zip(into, out):
        one.wait()
        two.start()
    for copy in out:
        copy.wait()


def local(inputs, out_grad, kernel_gate, inner_factor, outer_factor, chan_blocks, chan_mixers):
    full = jax.ShapeDtypeStruct((1024, 256), BF16)

    def buf(*shape, dtype=BF16):
        return pltpu.VMEM(shape, dtype)

    mixed, in_grad, kernel_grad = pl.pallas_call(
        kernel,
        out_shape=(full, full, full),
        in_specs=[pl.BlockSpec(memory_space=pl.ANY)] * 7,
        out_specs=[pl.BlockSpec(memory_space=pl.ANY)] * 3,
        scratch_shapes=[
            buf(ZH, 256, 256),
            buf(ZH, YC, 16, 256),
            buf(ZH, 256, 256),
            buf(ZH, YC, 16, 256),
            buf(1024, 256, dtype=F32),
            buf(1024, 256, dtype=F32),
            buf(1024, 256),
            buf(NQ, ZH, 64, 128),
            buf(NQ, ZH, 64, 128),
            buf(NQ, ZH, 64, 128),
            buf(PLANE, 64, 128),
            buf(ZH, YC, 16, 256),
            buf(ZH, YC, 16, 256),
            buf(YC, ZH, 16, 256),
            buf(ZH, NQ, 64, 128),
            buf(PLANE, 64, 128),
            buf(NQ, ZH, 64, 128),
            buf(NQ, ZH, 64, 128),
            buf(256, 256),
            buf(ZH, YC, 16, 256),
            buf(ZH, YC, 16, 256),
            buf(ZH, YC, 16, 256),
            buf(1024, 1024),
            buf(1024, 1024),
            buf(1024, 512),
            buf(64, 16, 256),
            buf(1024, 1024),
            buf(64, 64, dtype=F32),
            buf(1, 256, 256),
            buf(8, 8, 256),
            buf(64, 128, dtype=F32),
            buf(1024, 256),
            buf(1024, 256),
            buf(1024, 256),
            pltpu.SemaphoreType.DMA((10,)),
            pltpu.SemaphoreType.DMA((10, ZH)),
            pltpu.SemaphoreType.DMA((10,)),
            pltpu.SemaphoreType.DMA((9,)),
        ],
        compiler_params=pltpu.CompilerParams(
            collective_id=0, has_side_effects=True, vmem_limit_bytes=62 << 20
        ),
    )(
        inputs,
        out_grad,
        kernel_gate,
        inner_factor,
        outer_factor,
        chan_blocks,
        jnp.transpose(chan_mixers, (1, 2, 0)),
    )
    mixed, in_grad, kernel_grad = pl.pallas_call(
        hand_on,
        out_shape=(full, full, full),
        in_specs=[pl.BlockSpec(memory_space=pl.ANY)] * 3,
        out_specs=[pl.BlockSpec(memory_space=pl.ANY)] * 3,
        scratch_shapes=[buf(12, 256, 256), pltpu.SemaphoreType.DMA((12,)), pltpu.SemaphoreType.DMA((12,))],
        compiler_params=pltpu.CompilerParams(vmem_limit_bytes=62 << 20),
    )(mixed, in_grad, kernel_grad)
    return mixed, in_grad, kernel_grad.reshape(64, 16, 256)


def solution(mesh):
    in_specs = (
        P("seq", "chan"),
        P("seq", "chan"),
        P(None, "seq", "chan"),
        P(),
        P(),
        P("chan", None, None),
        P(),
    )
    out_specs = (P("seq", "chan"), P("seq", "chan"), P(None, "seq", "chan"))
    return jax.shard_map(local, mesh=mesh, in_specs=in_specs, out_specs=out_specs, check_vma=False)
```
